768 devices in a mesh: fsdp: 12 (over z), tp: 64 (over x, y, core).
Axes of the slice: x: 4, y: 8, z: 12, core: 2. Of those that a mesh axis runs over, the one named last changes fastest.
Arguments:
- weight: float32 [6144, 32768], P('fsdp', 'tp'), may hold values from -6 to 6
- momentum: float32 [6144, 32768], P('fsdp', 'tp'), may hold values from -54 to 54
- gradient: bfloat16 [6144, 32768], P('fsdp', 'tp'), may hold values from -6 to 6
- right_basis: float32 [32768, 256], P('tp'), may hold values from -6 to 6
Outputs:
- new_weight: float32 [6144, 32768], P('fsdp', 'tp')
- new_momentum: float32 [6144, 32768], P('fsdp', 'tp')
- new_right: float32 [32768, 256], P('tp')
The draws below stay inside these ranges and needn't reach their ends.
All inputs are finite; a program needn't handle non-finite values.
Results may differ from the reference program's by a relative error of at most 0.0003.
Values sent between devices are 32-bit elements; how exact they have to be, the bound alone decides.
No kernel may reach another device: no remote copies, remote signals or barrier semaphores. Data moves between devices by JAX's collectives and lax.ppermute only.
A program may use at most 32 MiB of HBM per device.

```python
import math
import jax
import jax.numpy as jnp
from jax import lax

ROWS = 6144
COLS = 32768
RANK = 256


def draw_momentum(key, part):
    key = jax.random.fold_in(key, 7)
    key_base, key_row, key_col = jax.random.split(key, 3)
    row_place = jnp.arange(ROWS, dtype=jnp.float32) / ROWS
    col_place = jnp.arange(COLS, dtype=jnp.float32) / COLS
    base = jnp.clip(jax.random.normal(key_base, (ROWS, COLS), jnp.float32), -6.0, 6.0)
    row_ramp = jnp.exp(math.log(3.0) * row_place)
    col_ramp = jnp.exp(math.log(3.0) * col_place)
    row_scale = jnp.exp(jax.random.uniform(key_row, (ROWS,), jnp.float32, math.log(0.2), 0.0)) * row_ramp
    col_scale = jnp.exp(jax.random.uniform(key_col, (COLS,), jnp.float32, math.log(0.2), 0.0)) * col_ramp
    return base * row_scale[:, None] * col_scale[None, :]


def block_scale(key, shape, pieces, least, largest):
    def one(axis_at, parts):
        draws = jax.random.uniform(jax.random.fold_in(jax.random.fold_in(key, 6), axis_at), (parts,), jnp.float32, least / len(pieces), largest / len(pieces))
        return jnp.repeat(jnp.exp(draws), shape[axis_at] // parts).reshape((-1,) + (1,) * (len(shape) - axis_at - 1))

    gain = one(*pieces[0])
    for cut in pieces[1:]:
        gain = gain * one(*cut)
    return gain


def noise(stream_key, dims, width, bound, cuts=(), held_as=jnp.bfloat16):
    drawn = width * jax.random.normal(stream_key, dims, jnp.float32)
    if cuts:
        drawn = drawn * block_scale(stream_key, dims, cuts, -0.22, 0.18)
    return jnp.clip(drawn, -bound, bound).astype(held_as)


def setup_inputs(seed: int = 0) -> dict:
    key_of = jax.random.split(jax.random.key(seed), 5)
    weight = noise(key_of[0], (ROWS, COLS), 1.0, 6.0, ((0, 12), (1, 64)), jnp.float32)
    momentum = draw_momentum(jax.random.fold_in(key_of[4], 71), 0)
    gradient = noise(key_of[2], (ROWS, COLS), 1.0, 6.0, ((0, 12), (1, 64)))
    right_basis = noise(key_of[3], (COLS, RANK), 1.0, 6.0, ((0, 64),), jnp.float32)
    return {"weight": weight, "momentum": momentum, "gradient": gradient, "right_basis": right_basis}


momentum_decay = 0.6
step_size = 2.0
epsilon_rms = 1e-06

def reference(weight, momentum, gradient, right_basis):
    highest = lax.Precision.HIGHEST
    buffer = momentum_decay * momentum + gradient.astype(jnp.float32)
    left_factor = jnp.dot(buffer, right_basis, precision=highest)
    gram_matrix = jnp.dot(left_factor.T, left_factor, precision=highest)
    factor = jnp.linalg.cholesky(gram_matrix)
    orthonormal = jax.scipy.linalg.solve_triangular(factor, left_factor.T, lower=True).T
    right_factor = jnp.dot(buffer.T, orthonormal, precision=highest)
    col_scale = lax.rsqrt(lax.optimization_barrier(jnp.sum(right_factor * right_factor, axis=0)) / COLS + epsilon_rms)
    new_right = right_factor * col_scale[None, :]
    new_momentum = buffer - (1.0 - momentum_decay) * jnp.dot(orthonormal, right_factor.T, precision=highest)
    new_weight = weight - step_size * jnp.dot(orthonormal, new_right.T, precision=highest)
    return (new_weight, new_momentum, new_right)
```

```python
import jax
import jax.numpy as jnp
from jax import lax
from jax.sharding import Mesh, PartitionSpec as P

COLS = 32768

momentum_decay = 0.6
step_size = 2.0
epsilon_rms = 1e-06

PLANE = ("x", "y")
TP = ("x", "y", "core")


def exchange(blocks, axes):
    return lax.all_to_all(blocks, axes, 0, 0)


def spread(block, axes, size):
    return exchange(jnp.broadcast_to(block[None], (size,) + block.shape), axes)


def body(weight, momentum, gradient, right_basis):
    highest = lax.Precision.HIGHEST
    nz, nxy = lax.axis_size("z"), lax.axis_size("x") * lax.axis_size("y")
    rows, cols = momentum.shape
    rank = right_basis.shape[1]
    buffer = momentum_decay * momentum + gradient.astype(jnp.float32)
    partial = jnp.dot(buffer, right_basis, precision=highest)
    half = exchange(partial.reshape(2, rows // 2, rank), "core").sum(0)
    share = exchange(half.reshape(nxy, rows // (2 * nxy), rank), PLANE).sum(0)
    half = spread(share, PLANE, nxy).reshape(rows // 2, rank)
    left_factor = lax.all_gather(half, "core", axis=0, tiled=True)
    gram = jnp.dot(left_factor.T, left_factor, precision=highest)
    turned = jnp.dot(buffer.T, left_factor, precision=highest)
    both = jnp.concatenate([turned, gram], axis=0)
    piece = exchange(both.reshape(nz, (cols + rank) // nz, rank), "z").sum(0)
    both = lax.all_gather(piece, "z", axis=0, tiled=True)
    turned, gram = both[:cols], both[cols:]
    factor = jnp.linalg.cholesky(gram)
    inverse = jax.scipy.linalg.solve_triangular(
        factor, jnp.eye(rank, dtype=jnp.float32), lower=True
    )
    right_factor = jnp.dot(turned, inverse.T, precision=highest)
    orthonormal = jnp.dot(left_factor, inverse.T, precision=highest)
    squares = jnp.sum(right_factor * right_factor, axis=0, keepdims=True)
    col_squares = spread(squares, TP, 2 * nxy).sum(0)
    col_scale = lax.rsqrt(col_squares / COLS + epsilon_rms)
    new_right = right_factor * col_scale
    new_momentum = buffer - (1.0 - momentum_decay) * jnp.dot(
        orthonormal, right_factor.T, precision=highest
    )
    new_weight = weight - step_size * jnp.dot(orthonormal, new_right.T, precision=highest)
    return (new_weight, new_momentum, new_right)


def solution(mesh):
    fine = Mesh(mesh.devices.reshape(mesh.devices.shape[0], 4, -1, 2), ("z", "x", "y", "core"))
    placed = (P("z", TP), P("z", TP), P("z", TP), P(TP, None))
    return jax.shard_map(
        body,
        mesh=fine,
        in_specs=placed,
        out_specs=(P("z", TP), P("z", TP), P(TP, None)),
        check_vma=False,
    )
```

```python
import jax
import jax.numpy as jnp
from jax import lax
from jax.experimental import pallas as pl
from jax.experimental.pallas import tpu as pltpu
from jax.sharding import Mesh, PartitionSpec as P

COLS = 32768

momentum_decay = 0.6
step_size = 2.0
epsilon_rms = 1e-06

PLANE = ("x", "y")
TP = ("x", "y", "core")


HIGHEST = lax.Precision.HIGHEST


def mul(a, b):
    return lax.dot_general(a, b, (((1,), (0,)), ((), ())), precision=HIGHEST, preferred_element_type=jnp.float32)


def mul_tn(a, b):
    return lax.dot_general(a, b, (((0,), (0,)), ((), ())), precision=HIGHEST, preferred_element_type=jnp.float32)


def mul_nt(a, b):
    return lax.dot_general(a, b, (((1,), (1,)), ((), ())), precision=HIGHEST, preferred_element_type=jnp.float32)


def inverse_factor(tiles):
    count = len(tiles)
    shape = tiles[0].shape
    lane = lax.broadcasted_iota(jnp.int32, shape, 1)
    sub = lax.broadcasted_iota(jnp.int32, shape, 0)
    out = []
    for k in range(count):
        first = 8 * k
        own = (lane >= first) & (lane < first + 8)
        top = tiles[k]
        cols = [jnp.broadcast_to(top[:, first + s : first + s + 1], shape) for s in range(8)]
        p = {
            (t, s): jnp.broadcast_to(cols[s][t : t + 1, :], shape)
            for s in range(8)
            for t in range(s, 8)
        }
        unit = jnp.where(own, jnp.where(lane == first + sub, 1.0, 0.0), top)
        row = [jnp.broadcast_to(unit[s : s + 1, :], shape) for s in range(8)]
        low, inv = {}, []
        for s in range(8):
            inv.append(1.0 / p[s, s])
            for t in range(s + 1, 8):
                low[t, s] = p[t, s] * inv[s]
            for t in range(s + 1, 8):
                for u in range(s + 1, t + 1):
                    p[t, u] = p[t, u] - low[t, s] * p[u, s]
                row[t] = row[t] - low[t, s] * row[s]
        done = row[0] * lax.rsqrt(p[0, 0])
        for s in range(1, 8):
            done = jnp.where(sub == s, row[s] * lax.rsqrt(p[s, s]), done)
        out.append(jnp.where(lane < first + 8, done, 0.0))
        if k + 1 == count:
            break
        back = [None] * 8
        for s in range(7, -1, -1):
            x = row[s] * inv[s]
            for t in range(7, s, -1):
                x = x - low[t, s] * back[t]
            back[s] = x
        for i in range(k + 1, count):
            tile = tiles[i]
            acc = jnp.where(own, 0.0, tile)
            for s in range(8):
                acc = acc - jnp.broadcast_to(tile[:, first + s : first + s + 1], shape) * back[s]
            tiles[i] = acc
    return out


def factor_into(gram, inv_ref, block_ref):
    n = block_ref.shape[1]

    def run(at):
        tiles = [block_ref[at, 8 * i : 8 * i + 8, :] for i in range(n // 8)]
        for i, tile in enumerate(inverse_factor(tiles)):
            block_ref[at, 8 * i : 8 * i + 8, :] = tile

    block_ref[0] = gram[:n, :n]
    block_ref[1] = gram[n:, n:]

    def step(at, carry):
        run(at)

        @pl.when(at == 0)
        def _():
            one = block_ref[0]
            cross = mul(one, gram[:n, n:])
            block_ref[1] = block_ref[1] - mul_tn(cross, cross)
            inv_ref[n:, :n] = mul_tn(cross, one)
        return carry

    lax.fori_loop(0, 2, step, 0)
    inv_ref[:n, :n] = block_ref[0]
    inv_ref[:n, n:] = jnp.zeros((n, n), jnp.float32)
    inv_ref[n:, n:] = block_ref[1]
    inv_ref[n:, :n] = -mul(block_ref[1], inv_ref[n:, :n])


def chol_kernel(gram_ref, inv_ref, block_ref):
    factor_into(gram_ref, inv_ref, block_ref)


def inverse_cholesky(gram):
    n = gram.shape[0]
    return pl.pallas_call(
        chol_kernel,
        out_shape=jax.ShapeDtypeStruct((n, n), jnp.float32),
        in_specs=[pl.BlockSpec(memory_space=pltpu.VMEM)],
        out_specs=pl.BlockSpec(memory_space=pltpu.VMEM),
        scratch_shapes=[pltpu.VMEM((2, n // 2, n // 2), jnp.float32)],
        compiler_params=pltpu.CompilerParams(vmem_limit_bytes=32 * 1024 * 1024),
    )(gram)


def exchange(blocks, axes):
    return lax.all_to_all(blocks, axes, 0, 0)


def spread(block, axes, size):
    return exchange(jnp.broadcast_to(block[None], (size,) + block.shape), axes)


def body(weight, momentum, gradient, right_basis):
    highest = lax.Precision.HIGHEST
    nz, nxy = lax.axis_size("z"), lax.axis_size("x") * lax.axis_size("y")
    rows, cols = momentum.shape
    rank = right_basis.shape[1]
    buffer = momentum_decay * momentum + gradient.astype(jnp.float32)
    partial = jnp.dot(buffer, right_basis, precision=highest)
    half = exchange(partial.reshape(2, rows // 2, rank), "core").sum(0)
    share = exchange(half.reshape(nxy, rows // (2 * nxy), rank), PLANE).sum(0)
    half = spread(share, PLANE, nxy).reshape(rows // 2, rank)
    left_factor = lax.all_gather(half, "core", axis=0, tiled=True)
    gram = jnp.dot(left_factor.T, left_factor, precision=highest)
    turned = jnp.dot(buffer.T, left_factor, precision=highest)
    both = jnp.concatenate([turned, gram], axis=0)
    piece = exchange(both.reshape(nz, (cols + rank) // nz, rank), "z").sum(0)
    both = lax.all_gather(piece, "z", axis=0, tiled=True)
    turned, gram = both[:cols], both[cols:]
    inverse = inverse_cholesky(gram)
    right_factor = jnp.dot(turned, inverse.T, precision=highest)
    orthonormal = jnp.dot(left_factor, inverse.T, precision=highest)
    squares = jnp.sum(right_factor * right_factor, axis=0, keepdims=True)
    col_squares = spread(squares, TP, 2 * nxy).sum(0)
    col_scale = lax.rsqrt(col_squares / COLS + epsilon_rms)
    new_right = right_factor * col_scale
    new_momentum = buffer - (1.0 - momentum_decay) * jnp.dot(
        orthonormal, right_factor.T, precision=highest
    )
    new_weight = weight - step_size * jnp.dot(orthonormal, new_right.T, precision=highest)
    return (new_weight, new_momentum, new_right)


def solution(mesh):
    fine = Mesh(mesh.devices.reshape(mesh.devices.shape[0], 4, -1, 2), ("z", "x", "y", "core"))
    placed = (P("z", TP), P("z", TP), P("z", TP), P(TP, None))
    return jax.shard_map(
        body,
        mesh=fine,
        in_specs=placed,
        out_specs=(P("z", TP), P("z", TP), P(TP, None)),
        check_vma=False,
    )
```

```python
import functools
import jax
import jax.numpy as jnp
from jax import lax
from jax.experimental import pallas as pl
from jax.experimental.pallas import tpu as pltpu
from jax.sharding import Mesh, PartitionSpec as P

COLS = 32768

momentum_decay = 0.6
step_size = 2.0
epsilon_rms = 1e-06

PLANE = ("x", "y")
TP = ("x", "y", "core")

HIGHEST = lax.Precision.HIGHEST


def mul(a, b):
    return lax.dot_general(a, b, (((1,), (0,)), ((), ())), precision=HIGHEST, preferred_element_type=jnp.float32)


def mul_tn(a, b):
    return lax.dot_general(a, b, (((0,), (0,)), ((), ())), precision=HIGHEST, preferred_element_type=jnp.float32)


def mul_nt(a, b):
    return lax.dot_general(a, b, (((1,), (1,)), ((), ())), precision=HIGHEST, preferred_element_type=jnp.float32)


def inverse_factor(tiles):
    count = len(tiles)
    shape = tiles[0].shape
    lane = lax.broadcasted_iota(jnp.int32, shape, 1)
    sub = lax.broadcasted_iota(jnp.int32, shape, 0)
    out = []
    for k in range(count):
        first = 8 * k
        own = (lane >= first) & (lane < first + 8)
        top = tiles[k]
        cols = [jnp.broadcast_to(top[:, first + s : first + s + 1], shape) for s in range(8)]
        p = {
            (t, s): jnp.broadcast_to(cols[s][t : t + 1, :], shape)
            for s in range(8)
            for t in range(s, 8)
        }
        unit = jnp.where(own, jnp.where(lane == first + sub, 1.0, 0.0), top)
        row = [jnp.broadcast_to(unit[s : s + 1, :], shape) for s in range(8)]
        low, inv = {}, []
        for s in range(8):
            inv.append(1.0 / p[s, s])
            for t in range(s + 1, 8):
                low[t, s] = p[t, s] * inv[s]
            for t in range(s + 1, 8):
                for u in range(s + 1, t + 1):
                    p[t, u] = p[t, u] - low[t, s] * p[u, s]
                row[t] = row[t] - low[t, s] * row[s]
        done = row[0] * lax.rsqrt(p[0, 0])
        for s in range(1, 8):
            done = jnp.where(sub == s, row[s] * lax.rsqrt(p[s, s]), done)
        out.append(jnp.where(lane < first + 8, done, 0.0))
        if k + 1 == count:
            break
        back = [None] * 8
        for s in range(7, -1, -1):
            x = row[s] * inv[s]
            for t in range(7, s, -1):
                x = x - low[t, s] * back[t]
            back[s] = x
        for i in range(k + 1, count):
            tile = tiles[i]
            acc = jnp.where(own, 0.0, tile)
            for s in range(8):
                acc = acc - jnp.broadcast_to(tile[:, first + s : first + s + 1], shape) * back[s]
            tiles[i] = acc
    return out


def halves_of(x):
    high = x.astype(jnp.bfloat16)
    return high, (x - high.astype(jnp.float32)).astype(jnp.bfloat16)


def right_kernel(top, both_ref, inv_ref, right_ref, sums_ref, block_ref, cross_ref, turned_ref):
    n = block_ref.shape[1]
    nz, low = both_ref.shape[0], both_ref.shape[1] - top
    cols = right_ref.shape[0]
    parts = (block_ref.at[0], cross_ref, block_ref.at[1])
    for at in range(nz):
        for i in range(0, low, 8):
            row = at * low + i
            if row < 3 * n:
                parts[row // n][row % n : row % n + 8, :] = both_ref[at, top + i : top + i + 8, :]
        stop = min(2 * cols, (at + 1) * top)
        if at * top < stop:
            turned_ref[at * top : stop, :] = both_ref[at, : stop - at * top, :]

    def step(at, carry):
        tiles = [block_ref[at, 8 * i : 8 * i + 8, :] for i in range(n // 8)]
        for i, tile in enumerate(inverse_factor(tiles)):
            block_ref[at, 8 * i : 8 * i + 8, :] = tile

        @pl.when(at == 0)
        def _():
            first = block_ref[0]
            cross = mul_nt(first, cross_ref[...])
            block_ref[1] = block_ref[1] - mul_tn(cross, cross)
            cross_ref[...] = mul_tn(cross, first)

        return carry

    lax.fori_loop(0, 2, step, 0)
    first, last = block_ref[0], block_ref[1]
    cross = -mul(last, cross_ref[...])
    inv_ref[:n, :n] = first
    inv_ref[:n, n:] = jnp.zeros((n, n), jnp.float32)
    inv_ref[n:, :n] = cross
    inv_ref[n:, n:] = last
    left, right = turned_ref[:cols, :], turned_ref[cols:, :]
    left, right = mul_nt(left, first), mul_nt(left, cross) + mul_nt(right, last)
    right_ref[:, :n] = left
    right_ref[:, n:] = right
    left = jnp.sum(left * left, axis=0, keepdims=True)
    right = jnp.sum(right * right, axis=0, keepdims=True)
    sums_ref[:, :, :n] = jnp.broadcast_to(left[None], (sums_ref.shape[0], 1, n))
    sums_ref[:, :, n:] = jnp.broadcast_to(right[None], (sums_ref.shape[0], 1, n))


def whole(kernel, shapes, scratch=(), limit=32, cost=(10**9, 2**22), **kw):
    return pl.pallas_call(
        kernel,
        out_shape=shapes,
        scratch_shapes=list(scratch),
        compiler_params=pltpu.CompilerParams(vmem_limit_bytes=limit * 1024 * 1024),
        cost_estimate=pl.CostEstimate(flops=cost[0], bytes_accessed=cost[1], transcendentals=0),
        **kw,
    )


def f32(*shape):
    return jax.ShapeDtypeStruct(shape, jnp.float32)


def turn_kernel(top, momentum_ref, gradient_ref, left_ref, out_ref):
    nz, both, n = out_ref.shape
    low = both - top
    cols = momentum_ref.shape[1]
    left = left_ref[...]
    square = mul_tn(left, left)
    blocks = (square[:n, :n], square[n:, :n], square[n:, n:])
    buffer = momentum_decay * momentum_ref[...] + gradient_ref[...].astype(jnp.float32)
    turned = mul_tn(buffer, left)
    for at in range(nz):
        for start, side in ((0, 0), (cols, 1)):
            lo, hi = max(at * top, start), min((at + 1) * top, start + cols)
            if lo < hi:
                out_ref[at, lo - at * top : hi - at * top, :] = turned[lo - start : hi - start, side * n : side * n + n]
        fill = max(2 * cols - at * top, 0)
        if fill < top:
            out_ref[at, fill:top, :] = jnp.zeros((top - fill, n), jnp.float32)
        for i in range(0, low, 8):
            row = at * low + i
            if row < 3 * n:
                out_ref[at, top + i : top + i + 8, :] = blocks[row // n][row % n : row % n + 8, :]
            else:
                out_ref[at, top + i : top + i + 8, :] = jnp.zeros((8, n), jnp.float32)


def products(a, b):
    head, tail = halves_of(a)
    high, low = halves_of(b)
    part = functools.partial(lax.dot_general, dimension_numbers=(((1,), (1,)), ((), ())), preferred_element_type=jnp.float32)
    return part(head, high) + (part(head, low) + part(tail, high))


def momentum_kernel(inv_ref, left_ref, right_ref, momentum_ref, gradient_ref, new_momentum_ref, basis_ref):
    basis = mul_nt(left_ref[...], inv_ref[...])
    basis_ref[...] = basis
    buffer = momentum_decay * momentum_ref[...] + gradient_ref[...].astype(jnp.float32)
    new_momentum_ref[...] = buffer - (1.0 - momentum_decay) * products(basis, right_ref[...])


def weight_kernel(sums_ref, weight_ref, basis_ref, right_ref, new_weight_ref, new_right_ref):
    scale = lax.rsqrt(jnp.sum(sums_ref[...], axis=0) / COLS + epsilon_rms)

    @pl.when(pl.program_id(0) == 0)
    def _():
        new_right_ref[...] = right_ref[...] * scale

    new_weight_ref[...] = weight_ref[...] - step_size * products(basis_ref[...], new_right_ref[...])


def weight_step(sums, weight, basis, right):
    rows, cols = weight.shape
    rank = right.shape[1]
    block = rows // 4
    whole_spec = pl.BlockSpec((cols, rank), lambda i: (0, 0))
    return whole(
        weight_kernel,
        (f32(rows, cols), f32(cols, rank)),
        grid=(rows // block,),
        in_specs=[
            pl.BlockSpec(sums.shape, lambda i: (0, 0, 0)),
            pl.BlockSpec((block, cols), lambda i: (i, 0)),
            pl.BlockSpec((block, rank), lambda i: (i, 0)),
            whole_spec,
        ],
        out_specs=(pl.BlockSpec((block, cols), lambda i: (i, 0)), whole_spec),
    )(sums, weight, basis, right)


def exchange(blocks, axes):
    return lax.all_to_all(blocks, axes, 0, 0)


def spread(block, axes, size):
    return exchange(jnp.broadcast_to(block[None], (size,) + block.shape), axes)


def body(weight, momentum, gradient, right_basis):
    highest = lax.Precision.HIGHEST
    nz, nxy = lax.axis_size("z"), lax.axis_size("x") * lax.axis_size("y")
    rows, cols = momentum.shape
    rank = right_basis.shape[1]
    buffer = momentum_decay * momentum + gradient.astype(jnp.float32)
    partial = jnp.dot(buffer, right_basis, precision=highest)
    half = exchange(partial.reshape(2, rows // 2, rank), "core").sum(0)
    share = exchange(half.reshape(nxy, rows // (2 * nxy), rank), PLANE).sum(0)
    half = spread(share, PLANE, nxy).reshape(rows // 2, rank)
    left_factor = lax.all_gather(half, "core", axis=0, tiled=True)
    half = rank // 2
    top = -(-2 * cols // (8 * nz)) * 8
    low = -(-3 * half // (8 * nz)) * 8
    pieces = whole(functools.partial(turn_kernel, top), f32(nz, top + low, half))(
        momentum, gradient, left_factor
    )
    piece = exchange(pieces, "z").sum(0)
    both = lax.all_gather(piece, "z")
    scratch = [(2, half, half), (half, half), (2 * cols, half)]
    inverse, right_factor, sums = whole(
        functools.partial(right_kernel, top),
        (f32(rank, rank), f32(cols, rank), f32(2 * nxy, 1, rank)),
        [pltpu.VMEM(shape, jnp.float32) for shape in scratch],
        cost=(10**10, 2**25),
    )(both)
    sums = exchange(sums, TP)
    new_momentum, orthonormal = whole(
        momentum_kernel, (f32(rows, cols), f32(rows, rank)), cost=(10**9, 2**24)
    )(inverse, left_factor, right_factor, momentum, gradient)
    new_weight, new_right = weight_step(sums, weight, orthonormal, right_factor)
    return (new_weight, new_momentum, new_right)


def solution(mesh):
    fine = Mesh(mesh.devices.reshape(mesh.devices.shape[0], 4, -1, 2), ("z", "x", "y", "core"))
    placed = (P("z", TP), P("z", TP), P("z", TP), P(TP, None))
    return jax.shard_map(
        body,
        mesh=fine,
        in_specs=placed,
        out_specs=(P("z", TP), P("z", TP), P(TP, None)),
        check_vma=False,
    )
```

```python
import functools
import jax
import jax.numpy as jnp
from jax import lax
from jax.experimental import pallas as pl
from jax.experimental.pallas import tpu as pltpu
from jax.sharding import Mesh, PartitionSpec as P

COLS = 32768

momentum_decay = 0.6
step_size = 2.0
epsilon_rms = 1e-06

PLANE = ("x", "y")
TP = ("x", "y", "core")

HIGHEST = lax.Precision.HIGHEST


def mul(a, b):
    return lax.dot_general(a, b, (((1,), (0,)), ((), ())), precision=HIGHEST, preferred_element_type=jnp.float32)


def mul_tn(a, b):
    return lax.dot_general(a, b, (((0,), (0,)), ((), ())), precision=HIGHEST, preferred_element_type=jnp.float32)


def mul_nt(a, b):
    return lax.dot_general(a, b, (((1,), (1,)), ((), ())), precision=HIGHEST, preferred_element_type=jnp.float32)


def inverse_factor(tiles, wide_ref):
    count = len(tiles)
    shape = tiles[0].shape
    lane = lax.broadcasted_iota(jnp.int32, shape, 1)
    sub = lax.broadcasted_iota(jnp.int32, shape, 0)
    out = []
    for k in range(count):
        first = 8 * k
        own = (lane >= first) & (lane < first + 8)
        top = tiles[k]
        cols = [jnp.broadcast_to(top[:, first + s : first + s + 1], shape) for s in range(8)]
        for s in range(8):
            wide_ref[k % 2, 8 * s : 8 * s + 8, :] = cols[s]
        unit = jnp.where(own, jnp.where(lane == first + sub, 1.0, 0.0), top)
        wide_ref[k % 2, 64:, :] = unit
        p = {(t, s): wide_ref[k % 2, pl.ds(8 * s + t, 8, stride=0), :] for s in range(8) for t in range(s, 8)}
        row = [wide_ref[k % 2, pl.ds(64 + s, 8, stride=0), :] for s in range(8)]
        low, inv = {}, []
        for s in range(8):
            inv.append(1.0 / p[s, s])
            for t in range(s + 1, 8):
                low[t, s] = p[t, s] * inv[s]
            for t in range(s + 1, 8):
                for u in range(s + 1, t + 1):
                    p[t, u] = p[t, u] - low[t, s] * p[u, s]
                row[t] = row[t] - low[t, s] * row[s]
        done = row[0] * lax.rsqrt(p[0, 0])
        for s in range(1, 8):
            done = jnp.where(sub == s, row[s] * lax.rsqrt(p[s, s]), done)
        out.append(jnp.where(lane < first + 8, done, 0.0))
        if k + 1 == count:
            break
        back = [None] * 8
        for s in range(7, -1, -1):
            x = row[s] * inv[s]
            for t in range(7, s, -1):
                x = x - low[t, s] * back[t]
            back[s] = x
        for i in range(k + 1, count):
            tile = tiles[i]
            acc = jnp.where(own, 0.0, tile)
            for s in range(7, -1, -1):
                acc = acc - jnp.broadcast_to(tile[:, first + s : first + s + 1], shape) * back[s]
            tiles[i] = acc
    return out


def halves_of(x):
    high = x.astype(jnp.bfloat16)
    return high, (x - high.astype(jnp.float32)).astype(jnp.bfloat16)


def right_kernel(top, both_ref, inv_ref, right_ref, sums_ref, block_ref, cross_ref, turned_ref, wide_ref):
    n = block_ref.shape[1]
    nz, low = both_ref.shape[0], both_ref.shape[1] - top
    cols = right_ref.shape[0]
    parts = (block_ref.at[0], cross_ref, block_ref.at[1])
    for at in range(nz):
        for i in range(0, low, 8):
            row = at * low + i
            if row < 3 * n:
                parts[row // n][row % n : row % n + 8, :] = both_ref[at, top + i : top + i + 8, :]
        stop = min(2 * cols, (at + 1) * top)
        if at * top < stop:
            turned_ref[at * top : stop, :] = both_ref[at, : stop - at * top, :]

    def step(at, carry):
        tiles = [block_ref[at, 8 * i : 8 * i + 8, :] for i in range(n // 8)]
        for i, tile in enumerate(inverse_factor(tiles, wide_ref)):
            block_ref[at, 8 * i : 8 * i + 8, :] = tile

        @pl.when(at == 0)
        def _():
            first = block_ref[0]
            cross = mul_nt(first, cross_ref[...])
            block_ref[1] = block_ref[1] - mul_tn(cross, cross)
            cross_ref[...] = mul_tn(cross, first)

        return carry

    lax.fori_loop(0, 2, step, 0)
    first, last = block_ref[0], block_ref[1]
    cross = -mul(last, cross_ref[...])
    inv_ref[:n, :n] = first
    inv_ref[:n, n:] = jnp.zeros((n, n), jnp.float32)
    inv_ref[n:, :n] = cross
    inv_ref[n:, n:] = last
    left, right = turned_ref[:cols, :], turned_ref[cols:, :]
    left, right = mul_nt(left, first), mul_nt(left, cross) + mul_nt(right, last)
    right_ref[:, :n] = left
    right_ref[:, n:] = right
    left = jnp.sum(left * left, axis=0, keepdims=True)
    right = jnp.sum(right * right, axis=0, keepdims=True)
    sums_ref[:, :, :n] = jnp.broadcast_to(left[None], (sums_ref.shape[0], 1, n))
    sums_ref[:, :, n:] = jnp.broadcast_to(right[None], (sums_ref.shape[0], 1, n))


def whole(kernel, shapes, scratch=(), limit=32, cost=(10**9, 2**22), **kw):
    return pl.pallas_call(
        kernel,
        out_shape=shapes,
        scratch_shapes=list(scratch),
        compiler_params=pltpu.CompilerParams(vmem_limit_bytes=limit * 1024 * 1024),
        cost_estimate=pl.CostEstimate(flops=cost[0], bytes_accessed=cost[1], transcendentals=0),
        **kw,
    )


def f32(*shape):
    return jax.ShapeDtypeStruct(shape, jnp.float32)


def turn_kernel(top, momentum_ref, gradient_ref, left_ref, out_ref):
    nz, both, n = out_ref.shape
    low = both - top
    cols = momentum_ref.shape[1]
    left = left_ref[...]
    square = mul_tn(left, left)
    blocks = (square[:n, :n], square[n:, :n], square[n:, n:])
    buffer = momentum_decay * momentum_ref[...] + gradient_ref[...].astype(jnp.float32)
    turned = mul_tn(buffer, left)
    for at in range(nz):
        for start, side in ((0, 0), (cols, 1)):
            lo, hi = max(at * top, start), min((at + 1) * top, start + cols)
            if lo < hi:
                out_ref[at, lo - at * top : hi - at * top, :] = turned[lo - start : hi - start, side * n : side * n + n]
        fill = max(2 * cols - at * top, 0)
        if fill < top:
            out_ref[at, fill:top, :] = jnp.zeros((top - fill, n), jnp.float32)
        for i in range(0, low, 8):
            row = at * low + i
            if row < 3 * n:
                out_ref[at, top + i : top + i + 8, :] = blocks[row // n][row % n : row % n + 8, :]
            else:
                out_ref[at, top + i : top + i + 8, :] = jnp.zeros((8, n), jnp.float32)


def products(a, halves):
    head, tail = halves_of(a)
    high, low = halves
    part = functools.partial(lax.dot_general, dimension_numbers=(((1,), (1,)), ((), ())), preferred_element_type=jnp.float32)
    return part(head, high) + (part(head, low) + part(tail, high))


def momentum_kernel(inv_ref, left_ref, right_ref, momentum_ref, gradient_ref, new_momentum_ref, basis_ref):
    basis = mul_nt(left_ref[...], inv_ref[...])
    basis_ref[...] = basis
    buffer = momentum_decay * momentum_ref[...] + gradient_ref[...].astype(jnp.float32)
    new_momentum_ref[...] = buffer - (1.0 - momentum_decay) * products(basis, halves_of(right_ref[...]))


def weight_kernel(sums_ref, weight_ref, basis_ref, right_ref, new_weight_ref, new_right_ref, block_ref, scaled_ref, in_sems, out_sems):
    count, size = block_ref.shape[:2]
    rows = [pl.ds(i * size, size) for i in range(count)]
    loads = [pltpu.make_async_copy(weight_ref.at[rows[i]], block_ref.at[i], in_sems.at[i]) for i in range(count)]
    stores = [pltpu.make_async_copy(block_ref.at[i], new_weight_ref.at[rows[i]], out_sems.at[i]) for i in range(count)]
    for load in loads:
        load.start()
    scale = lax.rsqrt(jnp.sum(sums_ref[...], axis=0) / COLS + epsilon_rms)
    new_right = right_ref[...] * scale
    scaled_ref[...] = new_right
    last = pltpu.make_async_copy(scaled_ref, new_right_ref, out_sems.at[count])
    last.start()
    scaled = halves_of(new_right)
    for i in range(count):
        product = products(basis_ref[rows[i], :], scaled)
        loads[i].wait()
        block_ref[i] = block_ref[i] - step_size * product
        stores[i].start()
    for store in stores:
        store.wait()
    last.wait()


def weight_step(sums, weight, basis, right):
    rows, cols = weight.shape
    rank = right.shape[1]
    count = 2
    vmem, anywhere = pl.BlockSpec(memory_space=pltpu.VMEM), pl.BlockSpec(memory_space=pl.ANY)
    return whole(
        weight_kernel,
        (f32(rows, cols), f32(cols, rank)),
        [
            pltpu.VMEM((count, rows // count, cols), jnp.float32),
            pltpu.VMEM((cols, rank), jnp.float32),
            pltpu.SemaphoreType.DMA((count,)),
            pltpu.SemaphoreType.DMA((count + 1,)),
        ],
        in_specs=[vmem, anywhere, vmem, vmem],
        limit=60,
        out_specs=(anywhere, anywhere),
    )(sums, weight, basis, right)


def exchange(blocks, axes):
    return lax.all_to_all(blocks, axes, 0, 0)


def spread(block, axes, size):
    return exchange(jnp.broadcast_to(block[None], (size,) + block.shape), axes)


def body(weight, momentum, gradient, right_basis):
    highest = lax.Precision.HIGHEST
    nz, nxy = lax.axis_size("z"), lax.axis_size("x") * lax.axis_size("y")
    rows, cols = momentum.shape
    rank = right_basis.shape[1]
    buffer = momentum_decay * momentum + gradient.astype(jnp.float32)
    partial = jnp.dot(buffer, right_basis, precision=highest)
    half = exchange(partial.reshape(2, rows // 2, rank), "core").sum(0)
    share = exchange(half.reshape(nxy, rows // (2 * nxy), rank), PLANE).sum(0)
    half = spread(share, PLANE, nxy).reshape(rows // 2, rank)
    left_factor = lax.all_gather(half, "core", axis=0, tiled=True)
    half = rank // 2
    top = -(-2 * cols // (8 * nz)) * 8
    low = -(-3 * half // (8 * nz)) * 8
    pieces = whole(functools.partial(turn_kernel, top), f32(nz, top + low, half))(
        momentum, gradient, left_factor
    )
    piece = exchange(pieces, "z").sum(0)
    both = lax.all_gather(piece, "z")
    scratch = [(2, half, half), (half, half), (2 * cols, half), (2, 72, half)]
    inverse, right_factor, sums = whole(
        functools.partial(right_kernel, top),
        (f32(rank, rank), f32(cols, rank), f32(2 * nxy, 1, rank)),
        [pltpu.VMEM(shape, jnp.float32) for shape in scratch],
        cost=(10**10, 2**25),
    )(both)
    sums = exchange(sums, TP)
    new_momentum, orthonormal = whole(
        momentum_kernel, (f32(rows, cols), f32(rows, rank)), cost=(10**9, 2**24)
    )(inverse, left_factor, right_factor, momentum, gradient)
    new_weight, new_right = weight_step(sums, weight, orthonormal, right_factor)
    return (new_weight, new_momentum, new_right)


def solution(mesh):
    fine = Mesh(mesh.devices.reshape(mesh.devices.shape[0], 4, -1, 2), ("z", "x", "y", "core"))
    placed = (P("z", TP), P("z", TP), P("z", TP), P(TP, None))
    return jax.shard_map(
        body,
        mesh=fine,
        in_specs=placed,
        out_specs=(P("z", TP), P("z", TP), P(TP, None)),
        check_vma=False,
    )
```

```python
import functools
import jax
import jax.numpy as jnp
from jax import lax
from jax.experimental import pallas as pl
from jax.experimental.pallas import tpu as pltpu
from jax.sharding import Mesh, PartitionSpec as P

COLS = 32768

momentum_decay = 0.6
step_size = 2.0
epsilon_rms = 1e-06

PLANE = ("x", "y")
TP = ("x", "y", "core")

HIGHEST = lax.Precision.HIGHEST


def mul(a, b):
    return lax.dot_general(a, b, (((1,), (0,)), ((), ())), precision=HIGHEST, preferred_element_type=jnp.float32)


def mul_tn(a, b):
    return lax.dot_general(a, b, (((0,), (0,)), ((), ())), precision=HIGHEST, preferred_element_type=jnp.float32)


def mul_nt(a, b):
    return lax.dot_general(a, b, (((1,), (1,)), ((), ())), precision=HIGHEST, preferred_element_type=jnp.float32)


def inverse_factor(tiles, wide_ref):
    count = len(tiles)
    shape = tiles[0].shape
    lane = lax.broadcasted_iota(jnp.int32, shape, 1)
    sub = lax.broadcasted_iota(jnp.int32, shape, 0)
    out = []
    for k in range(count):
        first = 8 * k
        own = (lane >= first) & (lane < first + 8)
        top = tiles[k]
        cols = [jnp.broadcast_to(top[:, first + s : first + s + 1], shape) for s in range(8)]
        for s in range(8):
            wide_ref[k % 2, 8 * s : 8 * s + 8, :] = cols[s]
        unit = jnp.where(own, jnp.where(lane == first + sub, 1.0, 0.0), top)
        wide_ref[k % 2, 64:, :] = unit
        p = {(t, s): wide_ref[k % 2, pl.ds(8 * s + t, 8, stride=0), :] for s in range(8) for t in range(s, 8)}
        row = [wide_ref[k % 2, pl.ds(64 + s, 8, stride=0), :] for s in range(8)]
        low, inv = {}, []
        for s in range(8):
            inv.append(1.0 / p[s, s])
            for t in range(s + 1, 8):
                low[t, s] = p[t, s] * inv[s]
            for t in range(s + 1, 8):
                for u in range(s + 1, t + 1):
                    p[t, u] = p[t, u] - low[t, s] * p[u, s]
                row[t] = row[t] - low[t, s] * row[s]
        done = row[0] * lax.rsqrt(p[0, 0])
        for s in range(1, 8):
            done = jnp.where(sub == s, row[s] * lax.rsqrt(p[s, s]), done)
        out.append(jnp.where(lane < first + 8, done, 0.0))
        if k + 1 == count:
            break
        back = [None] * 8
        for s in range(7, -1, -1):
            x = row[s] * inv[s]
            for t in range(7, s, -1):
                x = x - low[t, s] * back[t]
            back[s] = x
        for i in range(k + 1, count):
            tile = tiles[i]
            acc = jnp.where(own, 0.0, tile)
            for s in range(7, -1, -1):
                acc = acc - jnp.broadcast_to(tile[:, first + s : first + s + 1], shape) * back[s]
            tiles[i] = acc
    return out


def halves_of(x):
    high = x.astype(jnp.bfloat16)
    return high, (x - high.astype(jnp.float32)).astype(jnp.bfloat16)


def right_kernel(top, both_ref, inv_ref, right_ref, sums_ref, block_ref, cross_ref, turned_ref, wide_ref):
    n = block_ref.shape[1]
    nz, low = both_ref.shape[0], both_ref.shape[1] - top
    cols = right_ref.shape[0]
    parts = (block_ref.at[0], cross_ref, block_ref.at[1])
    low, half = low // 2, n // 2
    for at in range(nz):
        for i in range(0, low, 8):
            row = at * low + i
            if row < 3 * half:
                for core in range(2):
                    to, place = row % half + core * half, top + core * low + i
                    parts[row // half][to : to + 8, :] = both_ref[at, place : place + 8, :]
        stop = min(2 * cols, (at + 1) * top)
        if at * top < stop:
            turned_ref[at * top : stop, :] = both_ref[at, : stop - at * top, :]

    def step(at, carry):
        tiles = [block_ref[at, 8 * i : 8 * i + 8, :] for i in range(n // 8)]
        for i, tile in enumerate(inverse_factor(tiles, wide_ref)):
            block_ref[at, 8 * i : 8 * i + 8, :] = tile

        @pl.when(at == 0)
        def _():
            first = block_ref[0]
            cross = mul_nt(first, cross_ref[...])
            block_ref[1] = block_ref[1] - mul_tn(cross, cross)
            cross_ref[...] = mul_tn(cross, first)

        return carry

    lax.fori_loop(0, 2, step, 0)
    first, last = block_ref[0], block_ref[1]
    cross = -mul(last, cross_ref[...])
    inv_ref[:n, :n] = first
    inv_ref[:n, n:] = jnp.zeros((n, n), jnp.float32)
    inv_ref[n:, :n] = cross
    inv_ref[n:, n:] = last
    left, right = turned_ref[:cols, :], turned_ref[cols:, :]
    left, right = mul_nt(left, first), mul_nt(left, cross) + mul_nt(right, last)
    right_ref[:, :n] = left
    right_ref[:, n:] = right
    left = jnp.sum(left * left, axis=0, keepdims=True)
    right = jnp.sum(right * right, axis=0, keepdims=True)
    sums_ref[:, :, :n] = jnp.broadcast_to(left[None], (sums_ref.shape[0], 1, n))
    sums_ref[:, :, n:] = jnp.broadcast_to(right[None], (sums_ref.shape[0], 1, n))


def whole(kernel, shapes, scratch=(), limit=32, cost=(10**9, 2**22), **kw):
    return pl.pallas_call(
        kernel,
        out_shape=shapes,
        scratch_shapes=list(scratch),
        compiler_params=pltpu.CompilerParams(vmem_limit_bytes=limit * 1024 * 1024),
        cost_estimate=pl.CostEstimate(flops=cost[0], bytes_accessed=cost[1], transcendentals=0),
        **kw,
    )


def f32(*shape):
    return jax.ShapeDtypeStruct(shape, jnp.float32)


def turn_kernel(top, core_ref, momentum_ref, gradient_ref, left_ref, out_ref, gram_ref):
    nz, both, n = out_ref.shape
    low, half = both - top, n // 2
    cols = momentum_ref.shape[1]
    left = left_ref[...]
    square = mul_tn(left, left)
    gram_ref[:n, :] = square[:n, :n]
    gram_ref[n : 2 * n, :] = square[n:, :n]
    gram_ref[2 * n :, :] = square[n:, n:]
    mine = pl.multiple_of(core_ref[0] * half, half)
    blocks = [gram_ref[pl.ds(block * n + mine, half), :] for block in range(3)]
    buffer = momentum_decay * momentum_ref[...] + gradient_ref[...].astype(jnp.float32)
    turned = mul_tn(buffer, left)
    for at in range(nz):
        for start, side in ((0, 0), (cols, 1)):
            lo, hi = max(at * top, start), min((at + 1) * top, start + cols)
            if lo < hi:
                out_ref[at, lo - at * top : hi - at * top, :] = turned[lo - start : hi - start, side * n : side * n + n]
        fill = max(2 * cols - at * top, 0)
        if fill < top:
            out_ref[at, fill:top, :] = jnp.zeros((top - fill, n), jnp.float32)
        for i in range(0, low, 8):
            row = at * low + i
            if row < 3 * half:
                out_ref[at, top + i : top + i + 8, :] = blocks[row // half][row % half : row % half + 8, :]
            else:
                out_ref[at, top + i : top + i + 8, :] = jnp.zeros((8, n), jnp.float32)


def products(a, halves):
    head, tail = halves_of(a)
    high, low = halves
    part = functools.partial(lax.dot_general, dimension_numbers=(((1,), (1,)), ((), ())), preferred_element_type=jnp.float32)
    return part(head, high) + (part(head, low) + part(tail, high))


def momentum_kernel(inv_ref, left_ref, right_ref, momentum_ref, gradient_ref, new_momentum_ref, basis_ref):
    basis = mul_nt(left_ref[...], inv_ref[...])
    basis_ref[...] = basis
    buffer = momentum_decay * momentum_ref[...] + gradient_ref[...].astype(jnp.float32)
    new_momentum_ref[...] = buffer - (1.0 - momentum_decay) * products(basis, halves_of(right_ref[...]))


def weight_kernel(sums_ref, weight_ref, basis_ref, right_ref, new_weight_ref, new_right_ref, block_ref, scaled_ref, in_sems, out_sems):
    count, size = block_ref.shape[:2]
    rows = [pl.ds(i * size, size) for i in range(count)]
    loads = [pltpu.make_async_copy(weight_ref.at[rows[i]], block_ref.at[i], in_sems.at[i]) for i in range(count)]
    stores = [pltpu.make_async_copy(block_ref.at[i], new_weight_ref.at[rows[i]], out_sems.at[i]) for i in range(count)]
    for load in loads:
        load.start()
    scale = lax.rsqrt(jnp.sum(sums_ref[...], axis=0) / COLS + epsilon_rms)
    new_right = right_ref[...] * scale
    scaled_ref[...] = new_right
    last = pltpu.make_async_copy(scaled_ref, new_right_ref, out_sems.at[count])
    last.start()
    scaled = halves_of(new_right)
    for i in range(count):
        product = products(basis_ref[rows[i], :], scaled)
        loads[i].wait()
        block_ref[i] = block_ref[i] - step_size * product
        stores[i].start()
    for store in stores:
        store.wait()
    last.wait()


def weight_step(sums, weight, basis, right):
    rows, cols = weight.shape
    rank = right.shape[1]
    count = 2
    vmem, anywhere = pl.BlockSpec(memory_space=pltpu.VMEM), pl.BlockSpec(memory_space=pl.ANY)
    return whole(
        weight_kernel,
        (f32(rows, cols), f32(cols, rank)),
        [
            pltpu.VMEM((count, rows // count, cols), jnp.float32),
            pltpu.VMEM((cols, rank), jnp.float32),
            pltpu.SemaphoreType.DMA((count,)),
            pltpu.SemaphoreType.DMA((count + 1,)),
        ],
        in_specs=[vmem, anywhere, vmem, vmem],
        limit=60,
        out_specs=(anywhere, anywhere),
    )(sums, weight, basis, right)


def exchange(blocks, axes):
    return lax.all_to_all(blocks, axes, 0, 0)


def spread(block, axes, size):
    return exchange(jnp.broadcast_to(block[None], (size,) + block.shape), axes)


def body(weight, momentum, gradient, right_basis):
    highest = lax.Precision.HIGHEST
    nz, nxy = lax.axis_size("z"), lax.axis_size("x") * lax.axis_size("y")
    rows, cols = momentum.shape
    rank = right_basis.shape[1]
    core = lax.axis_index("core")

    def product(at):
        rows_of = functools.partial(lax.dynamic_slice_in_dim, start_index=at * (rows // 2), slice_size=rows // 2)
        buffer = momentum_decay * rows_of(momentum) + rows_of(gradient).astype(jnp.float32)
        return jnp.dot(buffer, right_basis, precision=highest)

    sent, own = lax.optimization_barrier(
        (lax.ppermute(product(1 - core), "core", [(0, 1), (1, 0)]), product(core))
    )
    half = sent + own
    share = exchange(half.reshape(nxy, rows // (2 * nxy), rank), PLANE).sum(0)
    half = spread(share, PLANE, nxy).reshape(rows // 2, rank)
    left_factor = lax.all_gather(half, "core", axis=0, tiled=True)
    half = rank // 2
    top = -(-2 * cols // (8 * nz)) * 8
    low = -(-3 * half // (16 * nz)) * 8
    vmem = pl.BlockSpec(memory_space=pltpu.VMEM)
    pieces = whole(
        functools.partial(turn_kernel, top),
        f32(nz, top + low, half),
        [pltpu.VMEM((3 * half, half), jnp.float32)],
        in_specs=[pl.BlockSpec(memory_space=pltpu.SMEM), vmem, vmem, vmem],
    )(core.reshape(1), momentum, gradient, left_factor)
    piece = exchange(pieces, "z").sum(0)
    shares = lax.all_gather(piece[top:], "core", axis=0, tiled=True)
    both = lax.all_gather(jnp.concatenate([piece[:top], shares], axis=0), "z")
    scratch = [(2, half, half), (half, half), (2 * cols, half), (2, 72, half)]
    inverse, right_factor, sums = whole(
        functools.partial(right_kernel, top),
        (f32(rank, rank), f32(cols, rank), f32(2 * nxy, 1, rank)),
        [pltpu.VMEM(shape, jnp.float32) for shape in scratch],
        cost=(10**10, 2**25),
    )(both)
    sums = exchange(sums, TP)
    new_momentum, orthonormal = whole(
        momentum_kernel, (f32(rows, cols), f32(rows, rank)), cost=(10**9, 2**24)
    )(inverse, left_factor, right_factor, momentum, gradient)
    new_weight, new_right = weight_step(sums, weight, orthonormal, right_factor)
    return (new_weight, new_momentum, new_right)


def solution(mesh):
    fine = Mesh(mesh.devices.reshape(mesh.devices.shape[0], 4, -1, 2), ("z", "x", "y", "core"))
    placed = (P("z", TP), P("z", TP), P("z", TP), P(TP, None))
    return jax.shard_map(
        body,
        mesh=fine,
        in_specs=placed,
        out_specs=(P("z", TP), P("z", TP), P(TP, None)),
        check_vma=False,
    )
```

```python
import functools
import jax
import jax.numpy as jnp
from jax import lax
from jax.experimental import pallas as pl
from jax.experimental.pallas import tpu as pltpu
from jax.sharding import Mesh, PartitionSpec as P

COLS = 32768

momentum_decay = 0.6
step_size = 2.0
epsilon_rms = 1e-06

PLANE = ("x", "y")
TP = ("x", "y", "core")

HIGHEST = lax.Precision.HIGHEST


def mul(a, b):
    return lax.dot_general(a, b, (((1,), (0,)), ((), ())), precision=HIGHEST, preferred_element_type=jnp.float32)


def mul_tn(a, b):
    return lax.dot_general(a, b, (((0,), (0,)), ((), ())), precision=HIGHEST, preferred_element_type=jnp.float32)


def mul_nt(a, b):
    return lax.dot_general(a, b, (((1,), (1,)), ((), ())), precision=HIGHEST, preferred_element_type=jnp.float32)


def inverse_factor(tiles, wide_ref):
    count = len(tiles)
    shape = tiles[0].shape
    lane = lax.broadcasted_iota(jnp.int32, shape, 1)
    sub = lax.broadcasted_iota(jnp.int32, shape, 0)
    out = []
    for k in range(count):
        first = 8 * k
        own = (lane >= first) & (lane < first + 8)
        top = tiles[k]
        cols = [jnp.broadcast_to(top[:, first + s : first + s + 1], shape) for s in range(8)]
        for s in range(8):
            wide_ref[k % 2, 8 * s : 8 * s + 8, :] = cols[s]
        unit = jnp.where(own, jnp.where(lane == first + sub, 1.0, 0.0), top)
        wide_ref[k % 2, 64:, :] = unit
        p = {(t, s): wide_ref[k % 2, pl.ds(8 * s + t, 8, stride=0), :] for s in range(8) for t in range(s, 8)}
        row = [wide_ref[k % 2, pl.ds(64 + s, 8, stride=0), :] for s in range(8)]
        low, inv = {}, []
        for s in range(8):
            inv.append(1.0 / p[s, s])
            for t in range(s + 1, 8):
                low[t, s] = p[t, s] * inv[s]
            for t in range(s + 1, 8):
                for u in range(s + 1, t + 1):
                    p[t, u] = p[t, u] - low[t, s] * p[u, s]
                row[t] = row[t] - low[t, s] * row[s]
        done = row[0] * lax.rsqrt(p[0, 0])
        for s in range(1, 8):
            done = jnp.where(sub == s, row[s] * lax.rsqrt(p[s, s]), done)
        out.append(jnp.where(lane < first + 8, done, 0.0))
        if k + 1 == count:
            break
        back = [None] * 8
        for s in range(7, -1, -1):
            x = row[s] * inv[s]
            for t in range(7, s, -1):
                x = x - low[t, s] * back[t]
            back[s] = x
        for i in range(k + 1, count):
            tile = tiles[i]
            acc = jnp.where(own, 0.0, tile)
            for s in range(7, -1, -1):
                acc = acc - jnp.broadcast_to(tile[:, first + s : first + s + 1], shape) * back[s]
            tiles[i] = acc
    return out


def halves_of(x):
    high = x.astype(jnp.bfloat16)
    return high, (x - high.astype(jnp.float32)).astype(jnp.bfloat16)


def right_kernel(top, both_ref, inv_ref, right_ref, sums_ref, block_ref, cross_ref, turned_ref, wide_ref):
    n = block_ref.shape[1]
    nz, low = both_ref.shape[0], both_ref.shape[1] - top
    cols = right_ref.shape[0]
    parts = (block_ref.at[0], cross_ref, block_ref.at[1])
    low, half = low // 2, n // 2
    for at in range(nz):
        for i in range(0, low, 8):
            row = at * low + i
            if row < 3 * half:
                for core in range(2):
                    to, place = row % half + core * half, top + core * low + i
                    parts[row // half][to : to + 8, :] = both_ref[at, place : place + 8, :]
        stop = min(2 * cols, (at + 1) * top)
        if at * top < stop:
            turned_ref[at * top : stop, :] = both_ref[at, : stop - at * top, :]

    def step(at, carry):
        tiles = [block_ref[at, 8 * i : 8 * i + 8, :] for i in range(n // 8)]
        for i, tile in enumerate(inverse_factor(tiles, wide_ref)):
            block_ref[at, 8 * i : 8 * i + 8, :] = tile

        @pl.when(at == 0)
        def _():
            first = block_ref[0]
            cross = mul_nt(first, cross_ref[...])
            block_ref[1] = block_ref[1] - mul_tn(cross, cross)
            cross_ref[...] = mul_tn(cross, first)

        return carry

    lax.fori_loop(0, 2, step, 0)
    first, last = block_ref[0], block_ref[1]
    cross = -mul(last, cross_ref[...])
    inv_ref[:n, :n] = first
    inv_ref[:n, n:] = jnp.zeros((n, n), jnp.float32)
    inv_ref[n:, :n] = cross
    inv_ref[n:, n:] = last
    left, right = turned_ref[:cols, :], turned_ref[cols:, :]
    left, right = mul_nt(left, first), mul_nt(left, cross) + mul_nt(right, last)
    right_ref[:, :n] = left
    right_ref[:, n:] = right
    left = jnp.sum(left * left, axis=0, keepdims=True)
    right = jnp.sum(right * right, axis=0, keepdims=True)
    sums_ref[:, :, :n] = jnp.broadcast_to(left[None], (sums_ref.shape[0], 1, n))
    sums_ref[:, :, n:] = jnp.broadcast_to(right[None], (sums_ref.shape[0], 1, n))


def whole(kernel, shapes, scratch=(), limit=32, cost=(10**9, 2**22), **kw):
    return pl.pallas_call(
        kernel,
        out_shape=shapes,
        scratch_shapes=list(scratch),
        compiler_params=pltpu.CompilerParams(vmem_limit_bytes=limit * 1024 * 1024),
        cost_estimate=pl.CostEstimate(flops=cost[0], bytes_accessed=cost[1], transcendentals=0),
        **kw,
    )


def f32(*shape):
    return jax.ShapeDtypeStruct(shape, jnp.float32)


def turn_kernel(top, core_ref, momentum_ref, gradient_ref, left_ref, out_ref, gram_ref):
    nz, both, n = out_ref.shape
    low, half = both - top, n // 2
    cols = momentum_ref.shape[1]
    left = left_ref[...]
    square = mul_tn(left, left)
    gram_ref[:n, :] = square[:n, :n]
    gram_ref[n : 2 * n, :] = square[n:, :n]
    gram_ref[2 * n :, :] = square[n:, n:]
    mine = pl.multiple_of(core_ref[0] * half, half)
    blocks = [gram_ref[pl.ds(block * n + mine, half), :] for block in range(3)]
    buffer = momentum_decay * momentum_ref[...] + gradient_ref[...].astype(jnp.float32)
    turned = mul_tn(buffer, left)
    for at in range(nz):
        for start, side in ((0, 0), (cols, 1)):
            lo, hi = max(at * top, start), min((at + 1) * top, start + cols)
            if lo < hi:
                out_ref[at, lo - at * top : hi - at * top, :] = turned[lo - start : hi - start, side * n : side * n + n]
        fill = max(2 * cols - at * top, 0)
        if fill < top:
            out_ref[at, fill:top, :] = jnp.zeros((top - fill, n), jnp.float32)
        for i in range(0, low, 8):
            row = at * low + i
            if row < 3 * half:
                out_ref[at, top + i : top + i + 8, :] = blocks[row // half][row % half : row % half + 8, :]
            else:
                out_ref[at, top + i : top + i + 8, :] = jnp.zeros((8, n), jnp.float32)


def products(a, halves):
    head, tail = halves_of(a)
    high, low = halves
    part = functools.partial(lax.dot_general, dimension_numbers=(((1,), (1,)), ((), ())), preferred_element_type=jnp.float32)
    return part(head, high) + (part(head, low) + part(tail, high))


def momentum_kernel(inv_ref, left_ref, right_ref, momentum_ref, gradient_ref, new_momentum_ref, basis_ref):
    basis = mul_nt(left_ref[...], inv_ref[...])
    basis_ref[...] = basis
    buffer = momentum_decay * momentum_ref[...] + gradient_ref[...].astype(jnp.float32)
    new_momentum_ref[...] = buffer - (1.0 - momentum_decay) * products(basis, halves_of(right_ref[...]))


def weight_kernel(*refs):
    sums_ref, weight_ref, basis_ref, right_ref, new_weight_ref, new_right_ref, block_ref, near_ref, basis_near, right_near = refs[:10]
    in_sems, out_sems = refs[10:]
    count, size = block_ref.shape[:2]
    rows = [pl.ds(i * size, size) for i in range(count)]
    pairs = [(sums_ref, near_ref), (right_ref, right_near), (basis_ref, basis_near)]
    pairs += [(weight_ref.at[rows[i]], block_ref.at[i]) for i in range(count)]
    loads = [pltpu.make_async_copy(*pair, in_sems.at[i]) for i, pair in enumerate(pairs)]
    for load in loads:
        load.start()
    stores = [pltpu.make_async_copy(block_ref.at[i], new_weight_ref.at[rows[i]], out_sems.at[i]) for i in range(count)]
    stores.append(pltpu.make_async_copy(right_near, new_right_ref, out_sems.at[count]))
    loads[0].wait()
    scale = lax.rsqrt(jnp.sum(near_ref[...], axis=0) / COLS + epsilon_rms)
    loads[1].wait()
    new_right = right_near[...] * scale
    right_near[...] = new_right
    stores[count].start()
    scaled = halves_of(new_right)
    loads[2].wait()
    for i in range(count):
        product = products(basis_near[rows[i], :], scaled)
        loads[3 + i].wait()
        block_ref[i] = block_ref[i] - step_size * product
        stores[i].start()
    for store in stores:
        store.wait()


def weight_step(sums, weight, basis, right):
    rows, cols = weight.shape
    rank = right.shape[1]
    count = 1
    anywhere = pl.BlockSpec(memory_space=pl.ANY)
    return whole(
        weight_kernel,
        (f32(rows, cols), f32(cols, rank)),
        [
            pltpu.VMEM((count, rows // count, cols), jnp.float32),
            pltpu.VMEM(sums.shape, jnp.float32),
            pltpu.VMEM(basis.shape, jnp.float32),
            pltpu.VMEM(right.shape, jnp.float32),
            pltpu.SemaphoreType.DMA((count + 3,)),
            pltpu.SemaphoreType.DMA((count + 1,)),
        ],
        limit=60,
        in_specs=[anywhere] * 4,
        out_specs=(anywhere, anywhere),
    )(sums, weight, basis, right)


def exchange(blocks, axes):
    return lax.all_to_all(blocks, axes, 0, 0)


def spread(block, axes, size):
    return exchange(jnp.broadcast_to(block[None], (size,) + block.shape), axes)


def body(weight, momentum, gradient, right_basis):
    highest = lax.Precision.HIGHEST
    nz, nxy = lax.axis_size("z"), lax.axis_size("x") * lax.axis_size("y")
    rows, cols = momentum.shape
    rank = right_basis.shape[1]
    core = lax.axis_index("core")

    def product(at):
        rows_of = functools.partial(lax.dynamic_slice_in_dim, start_index=at * (rows // 2), slice_size=rows // 2)
        buffer = momentum_decay * rows_of(momentum) + rows_of(gradient).astype(jnp.float32)
        return jnp.dot(buffer, right_basis, precision=highest)

    sent, own = lax.optimization_barrier(
        (lax.ppermute(product(1 - core), "core", [(0, 1), (1, 0)]), product(core))
    )
    half = sent + own
    share = exchange(half.reshape(nxy, rows // (2 * nxy), rank), PLANE).sum(0)
    half = spread(share, PLANE, nxy).reshape(rows // 2, rank)
    left_factor = lax.all_gather(half, "core", axis=0, tiled=True)
    half = rank // 2
    top = -(-2 * cols // (8 * nz)) * 8
    low = -(-3 * half // (16 * nz)) * 8
    vmem = pl.BlockSpec(memory_space=pltpu.VMEM)
    pieces = whole(
        functools.partial(turn_kernel, top),
        f32(nz, top + low, half),
        [pltpu.VMEM((3 * half, half), jnp.float32)],
        in_specs=[pl.BlockSpec(memory_space=pltpu.SMEM), vmem, vmem, vmem],
    )(core.reshape(1), momentum, gradient, left_factor)
    piece = exchange(pieces, "z").sum(0)
    shares = lax.all_gather(piece[top:], "core", axis=0, tiled=True)
    both = lax.all_gather(jnp.concatenate([piece[:top], shares], axis=0), "z")
    scratch = [(2, half, half), (half, half), (2 * cols, half), (2, 72, half)]
    inverse, right_factor, sums = whole(
        functools.partial(right_kernel, top),
        (f32(rank, rank), f32(cols, rank), f32(2 * nxy, 1, rank)),
        [pltpu.VMEM(shape, jnp.float32) for shape in scratch],
        cost=(10**10, 2**25),
    )(both)
    sums = exchange(sums, TP)
    new_momentum, orthonormal = whole(
        momentum_kernel, (f32(rows, cols), f32(rows, rank)), cost=(10**9, 2**24)
    )(inverse, left_factor, right_factor, momentum, gradient)
    new_weight, new_right = weight_step(sums, weight, orthonormal, right_factor)
    return (new_weight, new_momentum, new_right)


def solution(mesh):
    fine = Mesh(mesh.devices.reshape(mesh.devices.shape[0], 4, -1, 2), ("z", "x", "y", "core"))
    placed = (P("z", TP), P("z", TP), P("z", TP), P(TP, None))
    return jax.shard_map(
        body,
        mesh=fine,
        in_specs=placed,
        out_specs=(P("z", TP), P("z", TP), P(TP, None)),
        check_vma=False,
    )
```

```python
import functools
import jax
import jax.numpy as jnp
from jax import lax
from jax.experimental import pallas as pl
from jax.experimental.pallas import tpu as pltpu
from jax.sharding import Mesh, PartitionSpec as P

COLS = 32768

momentum_decay = 0.6
step_size = 2.0
epsilon_rms = 1e-06

PLANE = ("x", "y")
TP = ("x", "y", "core")

HIGHEST = lax.Precision.HIGHEST


def mul(a, b):
    return lax.dot_general(a, b, (((1,), (0,)), ((), ())), precision=HIGHEST, preferred_element_type=jnp.float32)


def mul_tn(a, b):
    return lax.dot_general(a, b, (((0,), (0,)), ((), ())), precision=HIGHEST, preferred_element_type=jnp.float32)


def mul_nt(a, b):
    return lax.dot_general(a, b, (((1,), (1,)), ((), ())), precision=HIGHEST, preferred_element_type=jnp.float32)


def inverse_factor(tiles, wide_ref):
    count = len(tiles)
    shape = tiles[0].shape
    lane = lax.broadcasted_iota(jnp.int32, shape, 1)
    sub = lax.broadcasted_iota(jnp.int32, shape, 0)
    out = []
    for k in range(count):
        first = 8 * k
        own = (lane >= first) & (lane < first + 8)
        top = tiles[k]
        cols = [jnp.broadcast_to(top[:, first + s : first + s + 1], shape) for s in range(8)]
        for s in range(8):
            wide_ref[k % 2, 8 * s : 8 * s + 8, :] = cols[s]
        unit = jnp.where(own, jnp.where(lane == first + sub, 1.0, 0.0), top)
        wide_ref[k % 2, 64:, :] = unit
        p = {(t, s): wide_ref[k % 2, pl.ds(8 * s + t, 8, stride=0), :] for s in range(8) for t in range(s, 8)}
        row = [wide_ref[k % 2, pl.ds(64 + s, 8, stride=0), :] for s in range(8)]
        low, inv = {}, []
        for s in range(8):
            inv.append(1.0 / p[s, s])
            for t in range(s + 1, 8):
                low[t, s] = p[t, s] * inv[s]
            for t in range(s + 1, 8):
                for u in range(s + 1, t + 1):
                    p[t, u] = p[t, u] - low[t, s] * p[u, s]
                row[t] = row[t] - low[t, s] * row[s]
        done = row[0] * lax.rsqrt(p[0, 0])
        for s in range(1, 8):
            done = jnp.where(sub == s, row[s] * lax.rsqrt(p[s, s]), done)
        out.append(jnp.where(lane < first + 8, done, 0.0))
        if k + 1 == count:
            break
        back = [None] * 8
        for s in range(7, -1, -1):
            x = row[s] * inv[s]
            for t in range(7, s, -1):
                x = x - low[t, s] * back[t]
            back[s] = x
        for i in range(k + 1, count):
            tile = tiles[i]
            acc = jnp.where(own, 0.0, tile)
            for s in range(7, -1, -1):
                acc = acc - jnp.broadcast_to(tile[:, first + s : first + s + 1], shape) * back[s]
            tiles[i] = acc
    return out


def halves_of(x):
    high = x.astype(jnp.bfloat16)
    return high, (x - high.astype(jnp.float32)).astype(jnp.bfloat16)


def right_kernel(top, both_ref, inv_ref, right_ref, sums_ref, block_ref, cross_ref, turned_ref, wide_ref):
    n = block_ref.shape[1]
    nz, low = both_ref.shape[0], both_ref.shape[1] - top
    cols = right_ref.shape[0]
    parts = (block_ref.at[0], cross_ref, block_ref.at[1])
    low, half = low // 2, n // 2
    for at in range(nz):
        for i in range(0, low, 8):
            row = at * low + i
            if row < 3 * half:
                for core in range(2):
                    to, place = row % half + core * half, top + core * low + i
                    parts[row // half][to : to + 8, :] = both_ref[at, place : place + 8, :]
        stop = min(2 * cols, (at + 1) * top)
        if at * top < stop:
            turned_ref[at * top : stop, :] = both_ref[at, : stop - at * top, :]

    def step(at, carry):
        tiles = [block_ref[at, 8 * i : 8 * i + 8, :] for i in range(n // 8)]
        for i, tile in enumerate(inverse_factor(tiles, wide_ref)):
            block_ref[at, 8 * i : 8 * i + 8, :] = tile

        @pl.when(at == 0)
        def _():
            first = block_ref[0]
            cross = mul_nt(first, cross_ref[...])
            block_ref[1] = block_ref[1] - mul_tn(cross, cross)
            cross_ref[...] = mul_tn(cross, first)

        return carry

    lax.fori_loop(0, 2, step, 0)
    first, last = block_ref[0], block_ref[1]
    cross = -mul(last, cross_ref[...])
    inv_ref[:n, :n] = first
    inv_ref[:n, n:] = jnp.zeros((n, n), jnp.float32)
    inv_ref[n:, :n] = cross
    inv_ref[n:, n:] = last
    left, right = turned_ref[:cols, :], turned_ref[cols:, :]
    left, right = mul_nt(left, first), mul_nt(left, cross) + mul_nt(right, last)
    right_ref[:, :n] = left
    right_ref[:, n:] = right
    left = jnp.sum(left * left, axis=0, keepdims=True)
    right = jnp.sum(right * right, axis=0, keepdims=True)
    sums_ref[:, :, :n] = jnp.broadcast_to(left[None], (sums_ref.shape[0], 1, n))
    sums_ref[:, :, n:] = jnp.broadcast_to(right[None], (sums_ref.shape[0], 1, n))


def whole(kernel, shapes, scratch=(), limit=32, cost=(10**9, 2**22), **kw):
    return pl.pallas_call(
        kernel,
        out_shape=shapes,
        scratch_shapes=list(scratch),
        compiler_params=pltpu.CompilerParams(vmem_limit_bytes=int(limit * 1024 * 1024)),
        cost_estimate=pl.CostEstimate(flops=cost[0], bytes_accessed=cost[1], transcendentals=0),
        **kw,
    )


def f32(*shape):
    return jax.ShapeDtypeStruct(shape, jnp.float32)


def product_kernel(half_ref, momentum_ref, gradient_ref, right_ref, out_ref, momentum_near, gradient_near, right_near, sems):
    size = out_ref.shape[0]
    rows = pl.ds(pl.multiple_of(half_ref[0] * size, size), size)
    pairs = [(right_ref, right_near), (momentum_ref.at[rows], momentum_near), (gradient_ref.at[rows], gradient_near)]
    loads = [pltpu.make_async_copy(*pair, sems.at[i]) for i, pair in enumerate(pairs)]
    for load in loads:
        load.start()
    for load in loads:
        load.wait()
    buffer = momentum_decay * momentum_near[...] + gradient_near[...].astype(jnp.float32)
    out_ref[...] = mul(buffer, right_near[...])


def product_of(half, momentum, gradient, right):
    rows, cols = momentum.shape
    rank = right.shape[1]
    anywhere = pl.BlockSpec(memory_space=pl.ANY)
    return whole(
        product_kernel,
        f32(rows // 2, rank),
        [
            pltpu.VMEM((rows // 2, cols), momentum.dtype),
            pltpu.VMEM((rows // 2, cols), gradient.dtype),
            pltpu.VMEM(right.shape, right.dtype),
            pltpu.SemaphoreType.DMA((3,)),
        ],
        limit=53.6,
        in_specs=[pl.BlockSpec(memory_space=pltpu.SMEM)] + [anywhere] * 3,
        out_specs=pl.BlockSpec(memory_space=pltpu.VMEM),
    )(half.reshape(1), momentum, gradient, right)


def turn_kernel(top, core_ref, momentum_ref, gradient_ref, left_ref, out_ref, gram_ref):
    nz, both, n = out_ref.shape
    low, half = both - top, n // 2
    cols = momentum_ref.shape[1]
    left = left_ref[...]
    square = mul_tn(left, left)
    gram_ref[:n, :] = square[:n, :n]
    gram_ref[n : 2 * n, :] = square[n:, :n]
    gram_ref[2 * n :, :] = square[n:, n:]
    mine = pl.multiple_of(core_ref[0] * half, half)
    blocks = [gram_ref[pl.ds(block * n + mine, half), :] for block in range(3)]
    buffer = momentum_decay * momentum_ref[...] + gradient_ref[...].astype(jnp.float32)
    turned = mul_tn(buffer, left)
    for at in range(nz):
        for start, side in ((0, 0), (cols, 1)):
            lo, hi = max(at * top, start), min((at + 1) * top, start + cols)
            if lo < hi:
                out_ref[at, lo - at * top : hi - at * top, :] = turned[lo - start : hi - start, side * n : side * n + n]
        fill = max(2 * cols - at * top, 0)
        if fill < top:
            out_ref[at, fill:top, :] = jnp.zeros((top - fill, n), jnp.float32)
        for i in range(0, low, 8):
            row = at * low + i
            if row < 3 * half:
                out_ref[at, top + i : top + i + 8, :] = blocks[row // half][row % half : row % half + 8, :]
            else:
                out_ref[at, top + i : top + i + 8, :] = jnp.zeros((8, n), jnp.float32)


def products(a, halves):
    head, tail = halves_of(a)
    high, low = halves
    part = functools.partial(lax.dot_general, dimension_numbers=(((1,), (1,)), ((), ())), preferred_element_type=jnp.float32)
    return part(head, high) + (part(head, low) + part(tail, high))


def momentum_kernel(inv_ref, left_ref, right_ref, momentum_ref, gradient_ref, new_momentum_ref, basis_ref):
    basis = mul_nt(left_ref[...], inv_ref[...])
    basis_ref[...] = basis
    buffer = momentum_decay * momentum_ref[...] + gradient_ref[...].astype(jnp.float32)
    new_momentum_ref[...] = buffer - (1.0 - momentum_decay) * products(basis, halves_of(right_ref[...]))


def weight_kernel(*refs):
    sums_ref, weight_ref, basis_ref, right_ref, new_weight_ref, new_right_ref, block_ref, near_ref, basis_near, right_near = refs[:10]
    in_sems, out_sems = refs[10:]
    count, size = block_ref.shape[:2]
    rows = [pl.ds(i * size, size) for i in range(count)]
    pairs = [(sums_ref, near_ref), (right_ref, right_near), (basis_ref, basis_near)]
    pairs += [(weight_ref.at[rows[i]], block_ref.at[i]) for i in range(count)]
    loads = [pltpu.make_async_copy(*pair, in_sems.at[i]) for i, pair in enumerate(pairs)]
    for load in loads:
        load.start()
    stores = [pltpu.make_async_copy(block_ref.at[i], new_weight_ref.at[rows[i]], out_sems.at[i]) for i in range(count)]
    stores.append(pltpu.make_async_copy(right_near, new_right_ref, out_sems.at[count]))
    loads[0].wait()
    scale = lax.rsqrt(jnp.sum(near_ref[...], axis=0) / COLS + epsilon_rms)
    loads[1].wait()
    new_right = right_near[...] * scale
    right_near[...] = new_right
    stores[count].start()
    scaled = halves_of(new_right)
    loads[2].wait()
    for i in range(count):
        product = products(basis_near[rows[i], :], scaled)
        loads[3 + i].wait()
        block_ref[i] = block_ref[i] - step_size * product
        stores[i].start()
    for store in stores:
        store.wait()


def weight_step(sums, weight, basis, right):
    rows, cols = weight.shape
    rank = right.shape[1]
    count = 1
    anywhere = pl.BlockSpec(memory_space=pl.ANY)
    return whole(
        weight_kernel,
        (f32(rows, cols), f32(cols, rank)),
        [
            pltpu.VMEM((count, rows // count, cols), jnp.float32),
            pltpu.VMEM(sums.shape, jnp.float32),
            pltpu.VMEM(basis.shape, jnp.float32),
            pltpu.VMEM(right.shape, jnp.float32),
            pltpu.SemaphoreType.DMA((count + 3,)),
            pltpu.SemaphoreType.DMA((count + 1,)),
        ],
        limit=53.6,
        in_specs=[anywhere] * 4,
        out_specs=(anywhere, anywhere),
    )(sums, weight, basis, right)


def exchange(blocks, axes):
    return lax.all_to_all(blocks, axes, 0, 0)


def spread(block, axes, size):
    return exchange(jnp.broadcast_to(block[None], (size,) + block.shape), axes)


def body(weight, momentum, gradient, right_basis):
    highest = lax.Precision.HIGHEST
    nz, nxy = lax.axis_size("z"), lax.axis_size("x") * lax.axis_size("y")
    rows, cols = momentum.shape
    rank = right_basis.shape[1]
    core = lax.axis_index("core")

    def product(at):
        rows_of = functools.partial(lax.dynamic_slice_in_dim, start_index=at * (rows // 2), slice_size=rows // 2)
        buffer = momentum_decay * rows_of(momentum) + rows_of(gradient).astype(jnp.float32)
        return jnp.dot(buffer, right_basis, precision=highest)

    other = product_of(1 - core, momentum, gradient, right_basis)
    sent, own = lax.optimization_barrier(
        (lax.ppermute(other, "core", [(0, 1), (1, 0)]), product(core))
    )
    half = sent + own
    share = exchange(half.reshape(nxy, rows // (2 * nxy), rank), PLANE).sum(0)
    half = spread(share, PLANE, nxy).reshape(rows // 2, rank)
    left_factor = lax.all_gather(half, "core", axis=0, tiled=True)
    half = rank // 2
    top = -(-2 * cols // (8 * nz)) * 8
    low = -(-3 * half // (16 * nz)) * 8
    vmem = pl.BlockSpec(memory_space=pltpu.VMEM)
    pieces = whole(
        functools.partial(turn_kernel, top),
        f32(nz, top + low, half),
        [pltpu.VMEM((3 * half, half), jnp.float32)],
        in_specs=[pl.BlockSpec(memory_space=pltpu.SMEM), vmem, vmem, vmem],
    )(core.reshape(1), momentum, gradient, left_factor)
    piece = exchange(pieces, "z").sum(0)
    shares = lax.all_gather(piece[top:], "core", axis=0, tiled=True)
    both = lax.all_gather(jnp.concatenate([piece[:top], shares], axis=0), "z")
    scratch = [(2, half, half), (half, half), (2 * cols, half), (2, 72, half)]
    inverse, right_factor, sums = whole(
        functools.partial(right_kernel, top),
        (f32(rank, rank), f32(cols, rank), f32(2 * nxy, 1, rank)),
        [pltpu.VMEM(shape, jnp.float32) for shape in scratch],
        cost=(10**10, 2**25),
    )(both)
    sums = exchange(sums, TP)
    new_momentum, orthonormal = whole(
        momentum_kernel, (f32(rows, cols), f32(rows, rank)), cost=(10**9, 2**24)
    )(inverse, left_factor, right_factor, momentum, gradient)
    new_weight, new_right = weight_step(sums, weight, orthonormal, right_factor)
    return (new_weight, new_momentum, new_right)


def solution(mesh):
    fine = Mesh(mesh.devices.reshape(mesh.devices.shape[0], 4, -1, 2), ("z", "x", "y", "core"))
    placed = (P("z", TP), P("z", TP), P("z", TP), P(TP, None))
    return jax.shard_map(
        body,
        mesh=fine,
        in_specs=placed,
        out_specs=(P("z", TP), P("z", TP), P(TP, None)),
        check_vma=False,
    )
```

```python
import functools
import jax
import jax.numpy as jnp
from jax import lax
from jax.experimental import pallas as pl
from jax.experimental.pallas import tpu as pltpu
from jax.sharding import Mesh, PartitionSpec as P

COLS = 32768

momentum_decay = 0.6
step_size = 2.0
epsilon_rms = 1e-06

PLANE = ("x", "y")
TP = ("x", "y", "core")

HIGHEST = lax.Precision.HIGHEST


def mul(a, b):
    return lax.dot_general(a, b, (((1,), (0,)), ((), ())), precision=HIGHEST, preferred_element_type=jnp.float32)


def mul_tn(a, b):
    return lax.dot_general(a, b, (((0,), (0,)), ((), ())), precision=HIGHEST, preferred_element_type=jnp.float32)


def mul_nt(a, b):
    return lax.dot_general(a, b, (((1,), (1,)), ((), ())), precision=HIGHEST, preferred_element_type=jnp.float32)


def inverse_factor(tiles, wide_ref):
    count = len(tiles)
    shape = tiles[0].shape
    lane = lax.broadcasted_iota(jnp.int32, shape, 1)
    sub = lax.broadcasted_iota(jnp.int32, shape, 0)
    out = []
    for k in range(count):
        first = 8 * k
        own = (lane >= first) & (lane < first + 8)
        top = tiles[k]
        cols = [jnp.broadcast_to(top[:, first + s : first + s + 1], shape) for s in range(8)]
        for s in range(8):
            wide_ref[k % 2, 8 * s : 8 * s + 8, :] = cols[s]
        unit = jnp.where(own, jnp.where(lane == first + sub, 1.0, 0.0), top)
        wide_ref[k % 2, 64:72, :] = unit
        p = {(t, s): wide_ref[k % 2, pl.ds(8 * s + t, 8, stride=0), :] for s in range(8) for t in range(s, 8)}
        row = [wide_ref[k % 2, pl.ds(64 + s, 8, stride=0), :] for s in range(8)]
        low, inv = {}, []
        for s in range(8):
            inv.append(1.0 / p[s, s])
            for t in range(s + 1, 8):
                low[t, s] = p[t, s] * inv[s]
            for t in range(s + 1, 8):
                for u in range(s + 1, t + 1):
                    p[t, u] = p[t, u] - low[t, s] * p[u, s]
                row[t] = row[t] - low[t, s] * row[s]
        done = row[0] * lax.rsqrt(p[0, 0])
        for s in range(1, 8):
            done = jnp.where(sub == s, row[s] * lax.rsqrt(p[s, s]), done)
        out.append(jnp.where(lane < first + 8, done, 0.0))
        if k + 1 == count:
            break
        back = [None] * 8
        for s in range(7, -1, -1):
            x = row[s] * inv[s]
            for t in range(7, s, -1):
                x = x - low[t, s] * back[t]
            back[s] = x
        for i in range(k + 1, count):
            tile = tiles[i]
            acc = jnp.where(own, 0.0, tile)
            for s in range(7, -1, -1):
                acc = acc - jnp.broadcast_to(tile[:, first + s : first + s + 1], shape) * back[s]
            tiles[i] = acc
    return out


def halves_of(x):
    high = x.astype(jnp.bfloat16)
    return high, (x - high.astype(jnp.float32)).astype(jnp.bfloat16)


def right_kernel(top, both_ref, inv_ref, right_ref, sums_ref, block_ref, cross_ref, turned_ref, wide_ref):
    n = block_ref.shape[1]
    nz, low = both_ref.shape[0], both_ref.shape[1] - top
    cols = right_ref.shape[0]
    parts = (block_ref.at[0], cross_ref, block_ref.at[1])
    low, half = low // 2, n // 2
    for at in range(nz):
        for i in range(0, low, 8):
            row = at * low + i
            if row < 3 * half:
                for core in range(2):
                    to, place = row % half + core * half, top + core * low + i
                    parts[row // half][to : to + 8, :] = both_ref[at, place : place + 8, :]
        stop = min(2 * cols, (at + 1) * top)
        if at * top < stop:
            turned_ref[at * top : stop, :] = both_ref[at, : stop - at * top, :]

    def step(at, carry):
        tiles = [block_ref[at, 8 * i : 8 * i + 8, :] for i in range(n // 8)]
        for i, tile in enumerate(inverse_factor(tiles, wide_ref)):
            block_ref[at, 8 * i : 8 * i + 8, :] = tile

        @pl.when(at == 0)
        def _():
            first = block_ref[0]
            cross = mul_nt(first, cross_ref[...])
            block_ref[1] = block_ref[1] - mul_tn(cross, cross)
            cross_ref[...] = mul_tn(cross, first)

        return carry

    lax.fori_loop(0, 2, step, 0)
    first, last = block_ref[0], block_ref[1]
    cross = -mul(last, cross_ref[...])
    inv_ref[:n, :n] = first
    inv_ref[:n, n:] = jnp.zeros((n, n), jnp.float32)
    inv_ref[n:, :n] = cross
    inv_ref[n:, n:] = last
    left, right = turned_ref[:cols, :], turned_ref[cols:, :]
    left, right = mul_nt(left, first), mul_nt(left, cross) + mul_nt(right, last)
    right_ref[:, :n] = left
    right_ref[:, n:] = right
    left = jnp.sum(left * left, axis=0, keepdims=True)
    right = jnp.sum(right * right, axis=0, keepdims=True)
    sums_ref[:, :, :n] = jnp.broadcast_to(left[None], (sums_ref.shape[0], 1, n))
    sums_ref[:, :, n:] = jnp.broadcast_to(right[None], (sums_ref.shape[0], 1, n))


def whole(kernel, shapes, scratch=(), limit=32, cost=(10**9, 2**22), **kw):
    return pl.pallas_call(
        kernel,
        out_shape=shapes,
        scratch_shapes=list(scratch),
        compiler_params=pltpu.CompilerParams(vmem_limit_bytes=int(limit * 1024 * 1024)),
        cost_estimate=pl.CostEstimate(flops=cost[0], bytes_accessed=cost[1], transcendentals=0),
        **kw,
    )


def f32(*shape):
    return jax.ShapeDtypeStruct(shape, jnp.float32)


def product_kernel(half_ref, momentum_ref, gradient_ref, right_ref, out_ref, momentum_near, gradient_near, right_near, sems):
    size = out_ref.shape[0]
    rows = pl.ds(pl.multiple_of(half_ref[0] * size, size), size)
    pairs = [(right_ref, right_near), (momentum_ref.at[rows], momentum_near), (gradient_ref.at[rows], gradient_near)]
    loads = [pltpu.make_async_copy(*pair, sems.at[i]) for i, pair in enumerate(pairs)]
    for load in loads:
        load.start()
    for load in loads:
        load.wait()
    buffer = momentum_decay * momentum_near[...] + gradient_near[...].astype(jnp.float32)
    out_ref[...] = mul(buffer, right_near[...])


def product_of(half, momentum, gradient, right):
    rows, cols = momentum.shape
    rank = right.shape[1]
    anywhere = pl.BlockSpec(memory_space=pl.ANY)
    return whole(
        product_kernel,
        f32(rows // 2, rank),
        [
            pltpu.VMEM((rows // 2, cols), momentum.dtype),
            pltpu.VMEM((rows // 2, cols), gradient.dtype),
            pltpu.VMEM(right.shape, right.dtype),
            pltpu.SemaphoreType.DMA((3,)),
        ],
        limit=53.6,
        in_specs=[pl.BlockSpec(memory_space=pltpu.SMEM)] + [anywhere] * 3,
        out_specs=pl.BlockSpec(memory_space=pltpu.VMEM),
    )(half.reshape(1), momentum, gradient, right)


def turn_kernel(top, core_ref, momentum_ref, gradient_ref, left_ref, out_ref, gram_ref):
    nz, both, n = out_ref.shape
    low, half = both - top, n // 2
    cols = momentum_ref.shape[1]
    left = left_ref[...]
    square = mul_tn(left, left)
    gram_ref[:n, :] = square[:n, :n]
    gram_ref[n : 2 * n, :] = square[n:, :n]
    gram_ref[2 * n :, :] = square[n:, n:]
    mine = pl.multiple_of(core_ref[0] * half, half)
    blocks = [gram_ref[pl.ds(block * n + mine, half), :] for block in range(3)]
    buffer = momentum_decay * momentum_ref[...] + gradient_ref[...].astype(jnp.float32)
    turned = mul_tn(buffer, left)
    for at in range(nz):
        for start, side in ((0, 0), (cols, 1)):
            lo, hi = max(at * top, start), min((at + 1) * top, start + cols)
            if lo < hi:
                out_ref[at, lo - at * top : hi - at * top, :] = turned[lo - start : hi - start, side * n : side * n + n]
        fill = max(2 * cols - at * top, 0)
        if fill < top:
            out_ref[at, fill:top, :] = jnp.zeros((top - fill, n), jnp.float32)
        for i in range(0, low, 8):
            row = at * low + i
            if row < 3 * half:
                out_ref[at, top + i : top + i + 8, :] = blocks[row // half][row % half : row % half + 8, :]
            else:
                out_ref[at, top + i : top + i + 8, :] = jnp.zeros((8, n), jnp.float32)


def products(a, halves):
    head, tail = halves_of(a)
    high, low = halves
    part = functools.partial(lax.dot_general, dimension_numbers=(((1,), (1,)), ((), ())), preferred_element_type=jnp.float32)
    return part(head, high) + (part(head, low) + part(tail, high))


def momentum_kernel(inv_ref, left_ref, right_ref, momentum_ref, gradient_ref, new_momentum_ref, basis_ref):
    basis = mul_nt(left_ref[...], inv_ref[...])
    basis_ref[...] = basis
    buffer = momentum_decay * momentum_ref[...] + gradient_ref[...].astype(jnp.float32)
    new_momentum_ref[...] = buffer - (1.0 - momentum_decay) * products(basis, halves_of(right_ref[...]))


def weight_kernel(*refs):
    sums_ref, weight_ref, basis_ref, right_ref, new_weight_ref, new_right_ref, block_ref, near_ref, basis_near, right_near = refs[:10]
    in_sems, out_sems = refs[10:]
    count, size = block_ref.shape[:2]
    rows = [pl.ds(i * size, size) for i in range(count)]
    pairs = [(sums_ref, near_ref), (right_ref, right_near), (basis_ref, basis_near)]
    pairs += [(weight_ref.at[rows[i]], block_ref.at[i]) for i in range(count)]
    loads = [pltpu.make_async_copy(*pair, in_sems.at[i]) for i, pair in enumerate(pairs)]
    for load in loads:
        load.start()
    stores = [pltpu.make_async_copy(block_ref.at[i], new_weight_ref.at[rows[i]], out_sems.at[i]) for i in range(count)]
    stores.append(pltpu.make_async_copy(right_near, new_right_ref, out_sems.at[count]))
    loads[0].wait()
    scale = lax.rsqrt(jnp.sum(near_ref[...], axis=0) / COLS + epsilon_rms)
    loads[1].wait()
    new_right = right_near[...] * scale
    right_near[...] = new_right
    stores[count].start()
    scaled = halves_of(new_right)
    loads[2].wait()
    for i in range(count):
        product = products(basis_near[rows[i], :], scaled)
        loads[3 + i].wait()
        block_ref[i] = block_ref[i] - step_size * product
        stores[i].start()
    for store in stores:
        store.wait()


def weight_step(sums, weight, basis, right):
    rows, cols = weight.shape
    rank = right.shape[1]
    count = 1
    anywhere = pl.BlockSpec(memory_space=pl.ANY)
    return whole(
        weight_kernel,
        (f32(rows, cols), f32(cols, rank)),
        [
            pltpu.VMEM((count, rows // count, cols), jnp.float32),
            pltpu.VMEM(sums.shape, jnp.float32),
            pltpu.VMEM(basis.shape, jnp.float32),
            pltpu.VMEM(right.shape, jnp.float32),
            pltpu.SemaphoreType.DMA((count + 3,)),
            pltpu.SemaphoreType.DMA((count + 1,)),
        ],
        limit=53.6,
        in_specs=[anywhere] * 4,
        out_specs=(anywhere, anywhere),
    )(sums, weight, basis, right)


def exchange(blocks, axes):
    return lax.all_to_all(blocks, axes, 0, 0)


def spread(block, axes, size):
    return exchange(jnp.broadcast_to(block[None], (size,) + block.shape), axes)


def body(weight, momentum, gradient, right_basis):
    highest = lax.Precision.HIGHEST
    nz, nxy = lax.axis_size("z"), lax.axis_size("x") * lax.axis_size("y")
    rows, cols = momentum.shape
    rank = right_basis.shape[1]
    core = lax.axis_index("core")

    def product(at):
        rows_of = functools.partial(lax.dynamic_slice_in_dim, start_index=at * (rows // 2), slice_size=rows // 2)
        buffer = momentum_decay * rows_of(momentum) + rows_of(gradient).astype(jnp.float32)
        return jnp.dot(buffer, right_basis, precision=highest)

    other = product_of(1 - core, momentum, gradient, right_basis)
    sent, own = lax.optimization_barrier(
        (lax.ppermute(other, "core", [(0, 1), (1, 0)]), product(core))
    )
    half = sent + own
    share = exchange(half.reshape(nxy, rows // (2 * nxy), rank), PLANE).sum(0)
    half = spread(share, PLANE, nxy).reshape(rows // 2, rank)
    left_factor = lax.all_gather(half, "core", axis=0, tiled=True)
    half = rank // 2
    top = -(-2 * cols // (8 * nz)) * 8
    low = -(-3 * half // (16 * nz)) * 8
    vmem = pl.BlockSpec(memory_space=pltpu.VMEM)
    pieces = whole(
        functools.partial(turn_kernel, top),
        f32(nz, top + low, half),
        [pltpu.VMEM((3 * half, half), jnp.float32)],
        in_specs=[pl.BlockSpec(memory_space=pltpu.SMEM), vmem, vmem, vmem],
    )(core.reshape(1), momentum, gradient, left_factor)
    piece = exchange(pieces, "z").sum(0)
    shares = lax.all_gather(piece[top:], "core", axis=0, tiled=True)
    both = lax.all_gather(jnp.concatenate([piece[:top], shares], axis=0), "z")
    scratch = [(2, half, half), (half, half), (2 * cols, half), (2, 80, half)]
    inverse, right_factor, sums = whole(
        functools.partial(right_kernel, top),
        (f32(rank, rank), f32(cols, rank), f32(2 * nxy, 1, rank)),
        [pltpu.VMEM(shape, jnp.float32) for shape in scratch],
        cost=(10**10, 2**25),
    )(both)
    sums = exchange(sums, TP)
    new_momentum, orthonormal = whole(
        momentum_kernel, (f32(rows, cols), f32(rows, rank)), cost=(10**9, 2**24)
    )(inverse, left_factor, right_factor, momentum, gradient)
    new_weight, new_right = weight_step(sums, weight, orthonormal, right_factor)
    return (new_weight, new_momentum, new_right)


def solution(mesh):
    fine = Mesh(mesh.devices.reshape(mesh.devices.shape[0], 4, -1, 2), ("z", "x", "y", "core"))
    placed = (P("z", TP), P("z", TP), P("z", TP), P(TP, None))
    return jax.shard_map(
        body,
        mesh=fine,
        in_specs=placed,
        out_specs=(P("z", TP), P("z", TP), P(TP, None)),
        check_vma=False,
    )
```
